32 devices in a mesh: dp: 4 (over y, x), ctx: 8 (over z, core).
Axes of the slice: x: 2, y: 2, z: 4, core: 2. Of those that a mesh axis runs over, the one named last changes fastest.
Arguments:
- tokens: bfloat16 [2, 4, 1024, 768], P(None, 'dp', 'ctx'), may hold values from -6 to 6
- lengths: int32 [2, 4], P(None, 'dp'), may hold values from 256 to 1024, as said below
- routes: int32 [2, 4, 1024, 2], P(None, 'dp', 'ctx'), may hold values from 0 to 3, all different within a row
- rel_table: int32 [1024], replicated, may hold values from 0 to 31
- rel_bias: float32 [32, 12], replicated, may hold values from -5 to 5
- cotangent: bfloat16 [2, 4, 1024, 768], P(None, 'dp', 'ctx'), may hold values from -6 to 6
- w_qkv: bfloat16 [768, 2304], P('dp'), may hold values from -0.21875 to 0.21875
- w_attn: bfloat16 [768, 768], P('dp'), may hold values from -2.5 to 2.5
- w_router: bfloat16 [768, 4], P('dp'), may hold values from -0.15625 to 0.15625
- gain_attn: bfloat16 [768], P('dp'), may hold values from 0.5 to 1.5
- gain_moe: bfloat16 [768], P('dp'), may hold values from 0.5 to 1.5
- w_expert_in: bfloat16 [4, 768, 3072], P(None, 'dp'), may hold values from -0.21875 to 0.21875
- w_expert_out: bfloat16 [4, 3072, 768], P(None, 'dp'), may hold values from -0.109375 to 0.109375
Outputs:
- output: bfloat16 [2, 4, 1024, 768], P(None, 'dp', 'ctx')
- d_tokens: bfloat16 [2, 4, 1024, 768], P(None, 'dp', 'ctx')
- d_w_qkv: float32 [768, 2304], P(('dp', 'ctx'))
- d_w_attn: float32 [768, 768], P(('dp', 'ctx'))
- d_w_router: float32 [768, 4], P(('dp', 'ctx'))
- d_gain_attn: float32 [768], P(('dp', 'ctx'))
- d_gain_moe: float32 [768], P(('dp', 'ctx'))
- d_w_expert_in: float32 [4, 768, 3072], P(None, ('dp', 'ctx'))
- d_w_expert_out: float32 [4, 3072, 768], P(None, ('dp', 'ctx'))
- d_rel_bias: float32 [384], P(('dp', 'ctx'))
The draws below stay inside these ranges and needn't reach their ends.
Inputs may be any that keep to these rules, and one draw needn't show every extreme that they name: `lengths`: for each sequence index one of the 2 micro-batches has length 1024. `routes`: the two experts of a slot differ.
All inputs are finite; a program needn't handle non-finite values.
Results may differ from the reference program's by a relative error of at most 0.028.
Values may be sent and summed in bfloat16 or wider, within the bound.
A program may use at most 512 MiB of HBM per device.

```python
import jax
import jax.numpy as jnp
from jax import lax

D = 768
H = 12
HD = 64
FF = 3072
E = 4
NB = 32
MB = 2
SEQ = 1024
SEQS = 4


def draw_lengths(key, part):
    key = jax.random.fold_in(key, 11)
    key_len, key_pick = jax.random.split(key)
    base = jax.random.randint(key_len, (MB, SEQS), SEQ // 4, SEQ + 1, dtype=jnp.int32)
    pick = jax.random.randint(key_pick, (1, SEQS), 0, MB, dtype=jnp.int32)
    rows = jnp.arange(MB, dtype=jnp.int32)[:, None]
    return jnp.where(rows == pick, SEQ, base).astype(jnp.int32)


def touch_ends(values, own_key, least, top_value):
    longest = values.shape.index(max(values.shape))
    spots = []
    for shift in (0, 1):
        where = [jax.random.randint(jax.random.fold_in(own_key, axis), (), 0, length) for axis, length in enumerate(values.shape)]
        where[longest] = (where[longest] + shift) % values.shape[longest]
        spots.append(tuple(where))
    return values.at[spots[0]].set(least).at[spots[1]].set(top_value)


def level_of(stream_key, dims, cuts, low, largest):
    def one(dim, parts):
        heights = jax.random.uniform(jax.random.fold_in(jax.random.fold_in(stream_key, 6), dim), (parts,), jnp.float32, low / len(cuts), largest / len(cuts))
        return jnp.repeat(jnp.exp(heights), dims[dim] // parts).reshape((-1,) + (1,) * (len(dims) - dim - 1))

    gain = one(*cuts[0])
    for cut in cuts[1:]:
        gain = gain * one(*cut)
    return gain


def picks_of(own_key, rows, number_of, top, lift):
    ranking = jax.random.permutation(jax.random.fold_in(own_key, 1), number_of)
    boost = ranking
    for power in range(3):
        boost = boost * boost // number_of
    boost = boost * lift // number_of
    chance = jax.random.randint(jax.random.fold_in(own_key, 2), (rows, number_of), 0, 4096) + boost
    fixed_rows = jax.random.permutation(jax.random.fold_in(own_key, 3), rows)[jnp.arange(number_of) % rows]
    chance = jnp.where(jnp.arange(rows)[:, None] == fixed_rows[None, :], 1 << 14, chance)
    priority = chance * number_of + jnp.arange(number_of)
    return lax.top_k(priority.astype(jnp.int32), top)[1].astype(jnp.int32)


def scatter_about(key, dims, spread, most, cuts=(), held_as=jnp.bfloat16):
    entries = jax.random.normal(key, dims, jnp.float32) * spread
    if len(cuts) > 0:
        entries = level_of(key, dims, cuts, -0.22, 0.18) * entries
    return jnp.clip(entries, min=-most, max=most).astype(held_as)


def setup_inputs(seed: int = 0) -> dict:
    arg_keys = jax.random.split(jax.random.key(seed), 14)
    tokens = scatter_about(arg_keys[0], (MB, SEQS, SEQ, D), 1.0, 6.0, ((1, 4), (2, 8)))
    lengths = draw_lengths(jax.random.fold_in(arg_keys[13], 71), 0)
    routes = picks_of(arg_keys[2], MB * SEQS * SEQ, E, 2, 4096).reshape((MB, SEQS, SEQ, 2))
    rel_table = touch_ends(jax.random.randint(arg_keys[3], (SEQ,), 0, NB), jax.random.fold_in(arg_keys[3], 1), 0, NB - 1).astype(jnp.int32)
    rel_bias = scatter_about(arg_keys[4], (NB, H), 1.0, 5.0, (), jnp.float32)
    cotangent = scatter_about(arg_keys[5], (MB, SEQS, SEQ, D), 1.0, 6.0, ((1, 4), (2, 8)))
    w_qkv = scatter_about(arg_keys[6], (D, 3 * D), D ** -0.5, 0.21875, ((0, 4),))
    w_attn = scatter_about(arg_keys[7], (D, D), 6 ** -0.5, 2.5, ((0, 4),))
    w_router = scatter_about(arg_keys[8], (D, E), (2 * D) ** -0.5, 0.15625, ((0, 4),))
    gain_attn = jnp.clip(1.0 + 0.1 * jax.random.normal(arg_keys[9], (D,), jnp.float32), 0.5, 1.5).astype(jnp.bfloat16)
    gain_moe = jnp.clip(1.0 + 0.1 * jax.random.normal(arg_keys[10], (D,), jnp.float32), 0.5, 1.5).astype(jnp.bfloat16)
    w_expert_in = scatter_about(arg_keys[11], (E, D, FF), D ** -0.5, 0.21875, ((1, 4),))
    w_expert_out = scatter_about(arg_keys[12], (E, FF, D), FF ** -0.5, 0.109375, ((1, 4),))
    return {"tokens": tokens, "lengths": lengths, "routes": routes, "rel_table": rel_table, "rel_bias": rel_bias, "cotangent": cotangent, "w_qkv": w_qkv, "w_attn": w_attn, "w_router": w_router, "gain_attn": gain_attn, "gain_moe": gain_moe, "w_expert_in": w_expert_in, "w_expert_out": w_expert_out}


EPSILON = 1e-06
NEGATIVE = -1e+30
HIGH = lax.Precision.HIGHEST

@jax.custom_vjp
def low(v):
    return lax.optimization_barrier(v.astype(jnp.bfloat16)).astype(jnp.float32)

@jax.custom_vjp
def low_back(v):
    return v

def low_keep(v):
    return (low(v), None)

def low_pass(kept, grad):
    return (grad,)

def back_keep(v):
    return (v, None)

def back_low(kept, grad):
    return (low(grad),)
low.defvjp(low_keep, low_pass)
low_back.defvjp(back_keep, back_low)

def dense(left, right):
    return jnp.dot(left, right, precision=HIGH)

def rms_scale(values):
    return lax.rsqrt(lax.optimization_barrier(jnp.mean(values * values, axis=-1, keepdims=True)) + EPSILON)

def layer(params, inputs, length, seq_routes, rel_table):
    w_qkv, w_attn, w_router, gain_attn, gain_moe, w_in, w_out, rel_bias = params
    span = inputs.shape[0]
    places = jnp.arange(span, dtype=jnp.int32)
    normed = low(inputs * rms_scale(inputs) * gain_attn)
    mixed = dense(normed, w_qkv)
    queries = low(low_back(mixed[:, :D])).reshape(span, H, HD)
    keys = low(low_back(mixed[:, D:2 * D])).reshape(span, H, HD)
    values = low(low_back(mixed[:, 2 * D:])).reshape(span, H, HD)
    buckets = (rel_table[:, None] == jnp.arange(NB, dtype=jnp.int32)[None, :]).astype(jnp.float32)
    dist_bias = dense(rel_bias.T, buckets.T)
    scale = HD ** (-0.5)
    block = min(span, 512)

    def attend(index):
        start = index * block
        query_block = lax.dynamic_slice_in_dim(queries, start, block, 0)
        query_pos = start + jnp.arange(block, dtype=jnp.int32)
        scores = jnp.einsum('qhd,khd->hqk', query_block, keys, precision=HIGH) * scale
        offsets = jnp.clip(query_pos[:, None] - places[None, :], 0, span - 1)
        scores = low_back(scores + jnp.take(dist_bias, offsets, axis=1))
        allowed = (places[None, :] <= query_pos[:, None]) & (places[None, :] < length)
        scores = jnp.where(allowed[None], scores, NEGATIVE)
        top = lax.optimization_barrier(jnp.max(scores, axis=-1, keepdims=True))
        weights = jnp.where(allowed[None], jnp.exp(scores - top), 0.0)
        probs = low(weights / lax.optimization_barrier(jnp.sum(weights, axis=-1, keepdims=True)))
        return jnp.einsum('hqk,khd->qhd', probs, values, precision=HIGH)
    attended = lax.map(jax.checkpoint(attend), jnp.arange(span // block, dtype=jnp.int32))
    attended = low(low_back(attended.reshape(span, D)))
    branch = low_back(dense(attended, w_attn))
    resid = inputs + branch
    normed_moe = low(resid * rms_scale(resid) * gain_moe)
    logits = low_back(dense(normed_moe, w_router))
    chosen = (seq_routes[:, :, None] == jnp.arange(E, dtype=jnp.int32)[None, None, :]).astype(jnp.float32)
    routed = lax.optimization_barrier(jnp.sum(chosen * logits[:, None, :], axis=-1))
    gates = jax.nn.softmax(routed, axis=-1)
    weight_all = lax.optimization_barrier(jnp.sum(chosen * gates[:, :, None], axis=1))
    total = resid
    for expert in range(E):
        hidden = low_back(dense(normed_moe, w_in[expert]))
        active = low(jax.nn.gelu(hidden, approximate=False))
        result = low_back(dense(active, w_out[expert]))
        total = total + weight_all[:, expert:expert + 1] * result
    return total

def reference(tokens, lengths, routes, rel_table, rel_bias, cotangent, w_qkv, w_attn, w_router, gain_attn, gain_moe, w_expert_in, w_expert_out):
    params = (w_qkv.astype(jnp.float32), w_attn.astype(jnp.float32), w_router.astype(jnp.float32), gain_attn.astype(jnp.float32), gain_moe.astype(jnp.float32), w_expert_in.astype(jnp.float32), w_expert_out.astype(jnp.float32), rel_bias.astype(jnp.float32))
    count = tokens.shape[0] * tokens.shape[1]
    flat_tokens = tokens.reshape(count, SEQ, D)
    flat_routes = routes.reshape(count, SEQ, 2)
    flat_cot = cotangent.reshape(count, SEQ, D)
    flat_lengths = lengths.reshape(count)
    zeros = jax.tree.map(jnp.zeros_like, params)

    def one(totals, item):
        seq_tokens, length, seq_routes, seq_cot = item
        valid = (jnp.arange(SEQ, dtype=jnp.int32) < length).astype(jnp.float32)
        output, pull = jax.vjp(lambda weights, inputs: layer(weights, inputs, length, seq_routes, rel_table), params, seq_tokens.astype(jnp.float32))
        grads, d_inputs = pull(seq_cot.astype(jnp.float32) * valid[:, None])
        totals = jax.tree.map(jnp.add, totals, grads)
        return (totals, (output.astype(jnp.bfloat16), d_inputs.astype(jnp.bfloat16)))
    totals, stacked = lax.scan(one, zeros, (flat_tokens, flat_lengths, flat_routes, flat_cot))
    outputs, d_inputs = stacked
    return (outputs.reshape(tokens.shape), d_inputs.reshape(tokens.shape), totals[0], totals[1], totals[2], totals[3], totals[4], totals[5], totals[6], totals[7].reshape(NB * H))
```

```python
import functools

import jax
import jax.numpy as jnp
from jax import lax
from jax.experimental import pallas as pl
from jax.experimental.pallas import tpu as pltpu
from jax.sharding import PartitionSpec as P

EPSILON = 1e-06
NEGATIVE = -1e30
HIGH = lax.Precision.HIGHEST
F32 = jnp.float32
BF16 = jnp.bfloat16
PLANE = ("dp", "core")
COLUMN = ("z", "core")
EVERY = ("dp", "z", "core")
VMEM_LIMIT = 60 * 1024 * 1024


def dot_nn(left, right):
    return lax.dot_general(left, right, (((1,), (0,)), ((), ())), preferred_element_type=F32)


def dot_nt(left, right):
    return lax.dot_general(left, right, (((1,), (1,)), ((), ())), preferred_element_type=F32)


def dot_tn(left, right):
    return lax.dot_general(left, right, (((0,), (0,)), ((), ())), preferred_element_type=F32)


def rms_scale(values):
    return lax.rsqrt(jnp.mean(values * values, axis=-1, keepdims=True) + EPSILON)


def norm_back(grad, scaled, gain, factor):
    inner = grad * gain
    return (
        factor * (inner - scaled * jnp.mean(inner * scaled, axis=-1, keepdims=True)),
        jnp.sum(grad * scaled, axis=0),
    )


def bias_tile(rd_ref, head, delta, span, block):
    low = span - (delta + 1) * block
    row = rd_ref[head : head + 1, low : low + 2 * block]
    wide = jnp.broadcast_to(row, (block, 2 * block))
    return pltpu.roll(wide, block + 1, 1, stride=1, stride_axis=0)[:, :block]


def allowed_tile(length, first_query, first_key, block):
    query = first_query + lax.broadcasted_iota(jnp.int32, (block, block), 0)
    key = first_key + lax.broadcasted_iota(jnp.int32, (block, block), 1)
    allowed = key < length
    if first_query == first_key:
        allowed = allowed & (key <= query)
    return allowed


def attend_kernel(
    len_ref, x_ref, gain_ref, w_ref, rd_ref, n1_ref, qkv_ref, o_ref, olow_ref, lse_ref, tb_ref,
    *, hg, hd, block, scale,
):
    span = x_ref.shape[0]
    count = span // block
    width = hg * hd
    length = len_ref[0]
    gain = gain_ref[...].astype(F32)
    for i in range(count):
        rows = slice(i * block, (i + 1) * block)
        x = x_ref[rows, :].astype(F32)
        n1 = (x * rms_scale(x) * gain).astype(BF16)
        n1_ref[rows, :] = n1
        qkv_ref[rows, :] = dot_nn(n1, w_ref[...]).astype(BF16)
    for head in range(hg):
        for delta in range(count):
            tb_ref[head, delta] = bias_tile(rd_ref, head, delta, span, block)
    lane = lax.broadcasted_iota(jnp.int32, (block, 128), 1)
    for i in range(count):
        rows = slice(i * block, (i + 1) * block)
        lse_all = jnp.zeros((block, 128), F32)
        outs = []
        for head in range(hg):
            cols = slice(head * hd, (head + 1) * hd)
            kcols = slice(width + head * hd, width + (head + 1) * hd)
            vcols = slice(2 * width + head * hd, 2 * width + (head + 1) * hd)
            q = qkv_ref[rows, cols]
            scores = []
            top = None
            for j in range(i + 1):
                keys = slice(j * block, (j + 1) * block)
                s = dot_nt(q, qkv_ref[keys, kcols]) * scale + tb_ref[head, i - j]
                s = jnp.where(allowed_tile(length, i * block, j * block, block), s, NEGATIVE)
                scores.append(s)
                peak = jnp.max(s, axis=-1, keepdims=True)
                top = peak if top is None else jnp.maximum(top, peak)
            total = jnp.zeros((block, 1), F32)
            accum = jnp.zeros((block, hd), F32)
            for j in range(i + 1):
                keys = slice(j * block, (j + 1) * block)
                weights = jnp.exp(scores[j] - top)
                total = total + jnp.sum(weights, axis=-1, keepdims=True)
                accum = accum + dot_nn(weights.astype(BF16), qkv_ref[keys, vcols])
            outs.append(accum / total)
            lse_all = jnp.where(lane == head, top + jnp.log(total), lse_all)
        out = jnp.concatenate(outs, axis=1)
        o_ref[rows, :] = out
        olow_ref[rows, :] = out.astype(BF16)
        lse_ref[rows, :] = lse_all


def vmem_specs(count):
    return [pl.BlockSpec(memory_space=pltpu.VMEM)] * count


def attend(length, x_all, gain, w, rd, hg, hd, scale):
    span, model = x_all.shape
    block = 256
    width = hg * hd
    return pl.pallas_call(
        functools.partial(attend_kernel, hg=hg, hd=hd, block=block, scale=scale),
        out_shape=(
            jax.ShapeDtypeStruct((span, model), BF16),
            jax.ShapeDtypeStruct((span, 3 * width), BF16),
            jax.ShapeDtypeStruct((span, width), F32),
            jax.ShapeDtypeStruct((span, width), BF16),
            jax.ShapeDtypeStruct((span, 128), F32),
        ),
        in_specs=[pl.BlockSpec(memory_space=pltpu.SMEM)] + vmem_specs(4),
        out_specs=tuple(vmem_specs(5)),
        scratch_shapes=[pltpu.VMEM((hg, span // block, block, block), F32)],
        compiler_params=pltpu.CompilerParams(vmem_limit_bytes=VMEM_LIMIT),
        name="attend",
    )(length, x_all, gain, w, rd)


def skew_sum(tile):
    rows, wide = tile.shape
    while rows > 1:
        half = rows // 2
        tile = tile[:half] + pltpu.roll(tile[half:], wide - half, 1)
        rows = half
    return tile


def attend_back_kernel(
    len_ref, n1_ref, qkv_ref, o_ref, lse_ref, do_ref, w_ref, rd_ref,
    dn1_ref, dw_ref, dd_ref, tb_ref, dt_ref, dacc_ref, dlow_ref,
    *, hg, hd, block, scale,
):
    span = n1_ref.shape[0]
    count = span // block
    width = hg * hd
    length = len_ref[0]
    for head in range(hg):
        for delta in range(count):
            tb_ref[head, delta] = bias_tile(rd_ref, head, delta, span, block)
    dt_ref[...] = jnp.zeros_like(dt_ref)
    dacc_ref[...] = jnp.zeros_like(dacc_ref)
    for i in range(count):
        rows = slice(i * block, (i + 1) * block)
        for head in range(hg):
            cols = slice(head * hd, (head + 1) * hd)
            kcols = slice(width + head * hd, width + (head + 1) * hd)
            vcols = slice(2 * width + head * hd, 2 * width + (head + 1) * hd)
            q = qkv_ref[rows, cols]
            do = do_ref[rows, cols]
            delta_sum = jnp.sum(do.astype(F32) * o_ref[rows, cols], axis=-1, keepdims=True)
            lse = lse_ref[rows, head : head + 1]
            dq = jnp.zeros((block, hd), F32)
            for j in range(i + 1):
                keys = slice(j * block, (j + 1) * block)
                k = qkv_ref[keys, kcols]
                s = dot_nt(q, k) * scale + tb_ref[head, i - j]
                p = jnp.exp(s - lse)
                p = jnp.where(allowed_tile(length, i * block, j * block, block), p, 0.0)
                dp = dot_nt(do, qkv_ref[keys, vcols])
                ds = (p * (dp - delta_sum)).astype(BF16)
                dt_ref[head, i - j] += ds.astype(F32)
                dq = dq + dot_nn(ds, k)
                dacc_ref[keys, kcols] += dot_tn(ds, q)
                dacc_ref[keys, vcols] += dot_tn(p.astype(BF16), do)
            dacc_ref[rows, cols] = dq
    for i in range(count):
        rows = slice(i * block, (i + 1) * block)
        dlow_ref[rows, : 2 * width] = (dacc_ref[rows, : 2 * width] * scale).astype(BF16)
        dlow_ref[rows, 2 * width :] = dacc_ref[rows, 2 * width :].astype(BF16)
        dn1_ref[rows, :] = dot_nt(dlow_ref[rows, :], w_ref[...]).astype(BF16)
    dw_ref[...] = dot_tn(n1_ref[...], dlow_ref[...]).astype(dw_ref.dtype)
    dd_ref[...] = jnp.zeros_like(dd_ref)
    for head in range(hg):
        for delta in range(count):
            low = span - (delta + 1) * block
            tile = jnp.concatenate(
                [dt_ref[head, delta], jnp.zeros((block, block), F32)], axis=1
            )
            row = pltpu.roll(skew_sum(tile), block - 1, 1)
            dd_ref[head : head + 1, low : low + 2 * block] += row


def attend_back(length, n1, qkv, o, lse, do, w, rd, hg, hd, scale):
    span, model = n1.shape
    block = 256
    width = hg * hd
    return pl.pallas_call(
        functools.partial(attend_back_kernel, hg=hg, hd=hd, block=block, scale=scale),
        out_shape=(
            jax.ShapeDtypeStruct((span, model), BF16),
            jax.ShapeDtypeStruct((model, 3 * width), BF16),
            jax.ShapeDtypeStruct((hg, span + block), F32),
        ),
        in_specs=[pl.BlockSpec(memory_space=pltpu.SMEM)] + vmem_specs(7),
        out_specs=tuple(vmem_specs(3)),
        scratch_shapes=[
            pltpu.VMEM((hg, span // block, block, block), F32),
            pltpu.VMEM((hg, span // block, block, block), F32),
            pltpu.VMEM((span, 3 * width), F32),
            pltpu.VMEM((span, 3 * width), BF16),
        ],
        compiler_params=pltpu.CompilerParams(vmem_limit_bytes=VMEM_LIMIT),
        name="attend_back",
    )(length, n1, qkv, o, lse, do, w, rd)


def gelu_parts(hidden):
    density = jnp.exp(-0.5 * hidden * hidden)
    t = 1.0 / (1.0 + (0.3275911 * 0.7071067811865476) * jnp.abs(hidden))
    poly = 1.061405429 * t - 1.453152027
    poly = poly * t + 1.421413741
    poly = poly * t - 0.284496736
    poly = poly * t + 0.254829592
    tail = 0.5 * poly * t * density
    phi = jnp.where(hidden >= 0.0, 1.0 - tail, tail)
    return hidden * phi, phi + hidden * density * 0.3989422804014327


def expert_kernel(
    n2_ref, dy_ref, c_ref, win_ref, wout_ref, y_ref, dn2_ref, dg_ref, dwin_ref, dwout_ref,
    awin_ref, awout_ref, *, experts, hidden_count,
):
    step = pl.program_id(0)
    last = pl.num_programs(0) - 1

    @pl.when(step == 0)
    def start():
        awin_ref[...] = jnp.zeros_like(awin_ref)
        awout_ref[...] = jnp.zeros_like(awout_ref)

    n2 = n2_ref[...]
    dy = dy_ref[...]
    c = c_ref[...]
    dgs = []
    y = None
    dn2 = None
    for e in range(experts):
        part = slice(e * hidden_count, (e + 1) * hidden_count)
        weight = c[:, e : e + 1]
        hidden = dot_nn(n2, win_ref[:, part])
        active, slope = gelu_parts(hidden)
        back = dot_nt(dy, wout_ref[part, :])
        dgs.append(jnp.sum(active * back, axis=-1, keepdims=True))
        mixed = (active * weight).astype(BF16)
        d_hidden = (back * weight * slope).astype(BF16)
        term = dot_nn(mixed, wout_ref[part, :])
        y = term if y is None else y + term
        term = dot_nt(d_hidden, win_ref[:, part])
        dn2 = term if dn2 is None else dn2 + term
        awout_ref[part, :] += dot_tn(mixed, dy)
        awin_ref[:, part] += dot_tn(n2, d_hidden)
    y_ref[...] = y.astype(BF16)
    dn2_ref[...] = dn2.astype(BF16)
    dg_ref[...] = jnp.concatenate(dgs, axis=1)

    @pl.when(step == last)
    def finish():
        dwin_ref[...] = awin_ref[...].astype(BF16)
        dwout_ref[...] = awout_ref[...].astype(BF16)


def expert_layer(n2, dy, c, win, wout, experts):
    count, model = n2.shape
    block = 256
    hidden_count = win.shape[1] // experts
    rows = pl.BlockSpec((block, model), lambda i: (i, 0))
    few = pl.BlockSpec((block, experts), lambda i: (i, 0))
    whole = pl.BlockSpec(memory_space=pltpu.VMEM)
    return pl.pallas_call(
        functools.partial(expert_kernel, experts=experts, hidden_count=hidden_count),
        out_shape=(
            jax.ShapeDtypeStruct((count, model), BF16),
            jax.ShapeDtypeStruct((count, model), BF16),
            jax.ShapeDtypeStruct((count, experts), F32),
            jax.ShapeDtypeStruct(win.shape, BF16),
            jax.ShapeDtypeStruct(wout.shape, BF16),
        ),
        grid=(count // block,),
        in_specs=[rows, rows, few, whole, whole],
        out_specs=(rows, rows, few, whole, whole),
        scratch_shapes=[pltpu.VMEM(win.shape, F32), pltpu.VMEM(wout.shape, F32)],
        compiler_params=pltpu.CompilerParams(vmem_limit_bytes=VMEM_LIMIT),
        name="experts",
    )(n2, dy, c, win, wout)


def local(
    tokens, lengths, routes, rel_table, rel_bias, cotangent, w_qkv, w_attn, w_router,
    gain_attn, gain_moe, w_expert_in, w_expert_out, *, ndp, nz,
):
    micro, _, slots, model = tokens.shape
    span = rel_table.shape[0]
    buckets_count, heads = rel_bias.shape
    hd = model // heads
    scale = hd ** (-0.5)
    experts = w_expert_in.shape[0]
    ff = w_expert_in.shape[2]
    hg = -(-heads // nz)
    pad_heads = hg * nz - heads
    width = hg * hd
    z = lax.axis_index("z")
    core = lax.axis_index("core")
    x_loc = tokens[:, 0]
    query_pos = (z * 2 + core) * slots + jnp.arange(slots, dtype=jnp.int32)
    valid = query_pos[None, :] < lengths
    dy_loc = jnp.where(valid[:, :, None], cotangent[:, 0], 0).reshape(micro * slots, model)

    x_all = lax.all_to_all(x_loc, "core", 0, 1, tiled=True)[0]
    x_all = lax.all_gather(x_all, "z", axis=0, tiled=True)
    wq = w_qkv.reshape(-1, 3, heads, hd)
    wq = jnp.pad(wq, ((0, 0), (0, 0), (0, pad_heads), (0, 0)))
    wq = lax.dynamic_slice_in_dim(wq, z * hg, hg, 2).reshape(-1, 3 * width)
    wq = lax.all_gather(wq, "dp", axis=0, tiled=True)
    wa = lax.all_gather(w_attn, "dp", axis=0, tiled=True)
    wr = lax.all_gather(w_router, "dp", axis=0, tiled=True)
    ga = lax.all_gather(gain_attn, "dp", axis=0, tiled=True)
    gm = lax.all_gather(gain_moe, "dp", axis=0, tiled=True)
    share = ff // (ndp * nz * 2)
    hidden_count = nz * share
    win = w_expert_in.reshape(experts, -1, ndp, nz, 2, share)
    win = lax.dynamic_index_in_dim(win, core, 4, keepdims=False)
    win = win.transpose(2, 1, 0, 3, 4).reshape(ndp, -1, experts * hidden_count)
    win = lax.all_to_all(win, "dp", 0, 0, tiled=True).reshape(model, experts * hidden_count)
    wout = w_expert_out.reshape(experts, nz, 2, share, model)
    wout = lax.dynamic_index_in_dim(wout, core, 2, keepdims=False)
    wout = wout.reshape(experts * hidden_count, model)
    dy = lax.all_gather(dy_loc, PLANE, axis=0, tiled=True)

    turned = rel_table[::-1]
    onehot = (turned[:, None] == jnp.arange(buckets_count, dtype=jnp.int32)[None, :]).astype(F32)
    bias_rows = jnp.pad(rel_bias.T, ((0, pad_heads), (0, 0)))
    bias_rows = lax.dynamic_slice_in_dim(bias_rows, z * hg, hg, 0)
    rd = lax.dot_general(bias_rows, onehot, (((1,), (1,)), ((), ())), precision=HIGH)
    rd = jnp.pad(rd, ((0, 0), (0, 256)))
    length = lax.dynamic_index_in_dim(lengths[:, 0], core, 0, keepdims=True)

    n1, qkv, o, olow, lse = attend(length, x_all, ga[None, :], wq, rd, hg, hd, scale)
    olow = olow.reshape(nz * 2, slots, width)
    olow = lax.all_to_all(olow, COLUMN, 0, 0, tiled=True)
    olow = olow.reshape(nz, 2, slots, width).transpose(1, 2, 0, 3)
    olow = olow.reshape(micro * slots, nz * width)[:, :model]

    x = x_loc.reshape(micro * slots, model).astype(F32)
    y1 = x + dot_nn(olow, wa)
    r2 = rms_scale(y1)
    z2 = y1 * r2
    gain_two = gm.astype(F32)
    n2 = (z2 * gain_two).astype(BF16)
    logits = dot_nn(n2, wr)
    chosen = (
        routes.reshape(micro * slots, 2)[:, :, None] == jnp.arange(experts)[None, None, :]
    ).astype(F32)
    routed = jnp.sum(chosen * logits[:, None, :], axis=-1)
    gates = jax.nn.softmax(routed, axis=-1)
    c = jnp.sum(chosen * gates[:, :, None], axis=1)

    n2_all = lax.all_gather(n2, PLANE, axis=0, tiled=True)
    c_all = lax.all_gather(c, PLANE, axis=0, tiled=True)
    y_part, dn2_part, dg_part, dwin, dwout = expert_layer(n2_all, dy, c_all, win, wout, experts)
    y = lax.psum_scatter(y_part, PLANE, scatter_dimension=0, tiled=True)
    dn2 = lax.psum_scatter(dn2_part, PLANE, scatter_dimension=0, tiled=True).astype(F32)
    dg = lax.psum_scatter(dg_part, PLANE, scatter_dimension=0, tiled=True)
    output = (y1 + y.astype(F32)).astype(BF16)

    d_routed_gate = jnp.sum(chosen * dg[:, None, :], axis=-1)
    d_routed = gates * (d_routed_gate - jnp.sum(gates * d_routed_gate, axis=-1, keepdims=True))
    d_logits = jnp.sum(chosen * d_routed[:, :, None], axis=1).astype(BF16)
    g_router = dot_tn(n2, d_logits)
    dn2 = dn2 + dot_nt(d_logits, wr)
    d_norm, g_gain_moe = norm_back(dn2, z2, gain_two, r2)
    dy1 = dy_loc.astype(F32) + d_norm
    dbr = dy1.astype(BF16)
    g_attn = dot_tn(olow, dbr).astype(BF16)
    do = dot_nt(dbr, wa).astype(BF16)
    do = jnp.pad(do, ((0, 0), (0, nz * width - model)))
    do = do.reshape(2, slots, nz, width).transpose(2, 0, 1, 3).reshape(nz * 2, slots, width)
    do = lax.all_to_all(do, COLUMN, 0, 0, tiled=True).reshape(span, width)

    dn1_part, g_qkv, dd = attend_back(length, n1, qkv, o, lse, do, wq, rd, hg, hd, scale)
    dn1 = dn1_part.reshape(nz, 1, 2 * slots, model)
    dn1 = lax.psum_scatter(dn1, "z", scatter_dimension=0, tiled=True)[0]
    dn1 = lax.all_to_all(dn1, "core", 1, 0, tiled=True).reshape(micro * slots, model).astype(F32)
    r1 = rms_scale(x)
    z1 = x * r1
    d_norm, g_gain_attn = norm_back(dn1, z1, ga.astype(F32), r1)
    d_tokens = (dy1 + d_norm).astype(BF16)

    piece = model // (ndp * nz * 2)
    g_out = lax.psum_scatter(
        dwout.reshape(experts, nz, share, model), "z", scatter_dimension=1, tiled=True
    ).reshape(experts, share, model).astype(F32)
    g_in = dwin.reshape(ndp, nz, 2, piece, experts * hidden_count)
    g_in = lax.psum_scatter(g_in, "z", scatter_dimension=1, tiled=True)
    g_in = g_in.reshape(ndp * 2, piece, experts * hidden_count)
    g_in = lax.all_to_all(g_in, PLANE, 0, 0, tiled=True)
    g_in = g_in.reshape(ndp, 2, piece, experts, nz, share).transpose(3, 2, 0, 4, 1, 5)
    g_in = g_in.reshape(experts, piece, ff).astype(F32)
    g_qkv = g_qkv.reshape(ndp, nz, 2, piece, 3 * width).transpose(0, 2, 1, 3, 4)
    g_qkv = g_qkv.reshape(ndp * 2, nz, piece, 3 * width)
    g_qkv = lax.psum_scatter(g_qkv, PLANE, scatter_dimension=0, tiled=True)[0]
    g_qkv = lax.all_to_all(g_qkv, "z", 0, 0, tiled=True)
    g_qkv = g_qkv.reshape(nz, piece, 3, width).transpose(1, 2, 0, 3).reshape(piece, 3, nz * width)
    g_qkv = g_qkv[:, :, :model].reshape(piece, 3 * model).astype(F32)
    g_attn = lax.psum_scatter(g_attn, EVERY, scatter_dimension=0, tiled=True).astype(F32)

    d_dist = dd[:, :span]
    g_bias = lax.dot_general(onehot, d_dist, (((0,), (1,)), ((), ())), precision=HIGH)
    spread = jnp.zeros((buckets_count, nz * hg), F32)
    g_bias = lax.dynamic_update_slice_in_dim(spread, g_bias, z * hg, 1)[:, :heads].reshape(-1)
    small = jnp.concatenate([g_router.reshape(-1), g_gain_attn, g_gain_moe, g_bias])
    small = lax.psum(small, EVERY)
    place = (lax.axis_index("dp") * nz + z) * 2 + core

    def own(first, count, rows):
        return lax.dynamic_slice_in_dim(small, first + place * rows, rows, 0)

    g_router = own(0, 0, piece * experts).reshape(piece, experts)
    g_gain_attn = own(model * experts, 0, piece)
    g_gain_moe = own(model * (experts + 1), 0, piece)
    each = buckets_count * heads // (ndp * nz * 2)
    g_bias = own(model * (experts + 2), 0, each)
    return (
        output.reshape(micro, 1, slots, model),
        d_tokens.reshape(micro, 1, slots, model),
        g_qkv, g_attn, g_router, g_gain_attn, g_gain_moe, g_in, g_out, g_bias,
    )


def solution(mesh):
    devices = mesh.devices
    ndp, nctx = devices.shape
    nz = nctx // 2
    sub = jax.sharding.Mesh(devices.reshape(ndp, nz, 2), EVERY)
    in_specs = (
        P(None, "dp", COLUMN, None),
        P(None, "dp"),
        P(None, "dp", COLUMN, None),
        P(),
        P(),
        P(None, "dp", COLUMN, None),
        P("dp", None),
        P("dp", None),
        P("dp", None),
        P("dp"),
        P("dp"),
        P(None, "dp", None),
        P(None, "dp", None),
    )
    out_specs = (
        P(None, "dp", COLUMN, None),
        P(None, "dp", COLUMN, None),
        P(EVERY, None),
        P(EVERY, None),
        P(EVERY, None),
        P(EVERY),
        P(EVERY),
        P(None, EVERY, None),
        P(None, EVERY, None),
        P(EVERY),
    )
    return jax.shard_map(
        functools.partial(local, ndp=ndp, nz=nz), mesh=sub,
        in_specs=in_specs, out_specs=out_specs, check_vma=False,
    )
```

```python
import functools

import jax
import jax.numpy as jnp
from jax import lax
from jax.experimental import pallas as pl
from jax.experimental.pallas import tpu as pltpu
from jax.sharding import PartitionSpec as P

EPSILON = 1e-06
NEGATIVE = -1e30
HIGH = lax.Precision.HIGHEST
F32 = jnp.float32
BF16 = jnp.bfloat16
PLANE = ("dp", "core")
COLUMN = ("z", "core")
EVERY = ("dp", "z", "core")
VMEM_LIMIT = 60 * 1024 * 1024


def dot_nn(left, right):
    return lax.dot_general(left, right, (((1,), (0,)), ((), ())), preferred_element_type=F32)


def dot_nt(left, right):
    return lax.dot_general(left, right, (((1,), (1,)), ((), ())), preferred_element_type=F32)


def dot_tn(left, right):
    return lax.dot_general(left, right, (((0,), (0,)), ((), ())), preferred_element_type=F32)


def rms_scale(values):
    return lax.rsqrt(jnp.mean(values * values, axis=-1, keepdims=True) + EPSILON)


def norm_back(grad, scaled, gain, factor):
    inner = grad * gain
    return (
        factor * (inner - scaled * jnp.mean(inner * scaled, axis=-1, keepdims=True)),
        jnp.sum(grad * scaled, axis=0),
    )


def bias_tile(rd_ref, head, delta, span, block):
    low = span - (delta + 1) * block
    row = rd_ref[head : head + 1, low : low + 2 * block]
    wide = jnp.broadcast_to(row, (block, 2 * block))
    return pltpu.roll(wide, block + 1, 1, stride=1, stride_axis=0)[:, :block]


def allowed_tile(length, first_query, first_key, block):
    query = first_query + lax.broadcasted_iota(jnp.int32, (block, block), 0)
    key = first_key + lax.broadcasted_iota(jnp.int32, (block, block), 1)
    allowed = key < length
    if first_query == first_key:
        allowed = allowed & (key <= query)
    return allowed


MESH = pl.DeviceIdType.MESH


def xor(left, right):
    out = 0
    bit = 1
    while bit <= right:
        here = lax.rem(lax.div(left, jnp.int32(bit)), jnp.int32(2))
        out = out + bit * (1 - here if right & bit else here)
        bit *= 2
    return out + lax.div(left, jnp.int32(bit)) * bit


def remote(source, target, send, receive, dp, z, core):
    return pltpu.make_async_remote_copy(
        src_ref=source, dst_ref=target, send_sem=send, recv_sem=receive,
        device_id={"dp": dp, "z": z, "core": core}, device_id_type=MESH,
    )


def gate_weights(logits, routes, experts):
    lane = lax.broadcasted_iota(jnp.int32, logits.shape, 1).astype(F32)
    first = lane == routes[:, 0:1]
    second = lane == routes[:, 1:2]
    one = jnp.sum(jnp.where(first, logits, 0.0), axis=-1, keepdims=True)
    two = jnp.sum(jnp.where(second, logits, 0.0), axis=-1, keepdims=True)
    top = jnp.maximum(one, two)
    one = jnp.exp(one - top)
    two = jnp.exp(two - top)
    scale = 1.0 / (one + two)
    return jnp.where(first, one * scale, 0.0) + jnp.where(second, two * scale, 0.0)


def front_kernel(
    len_ref, x_ref, cot_ref, route_ref, rd_ref, wq_l, wa_l, small_l, win_h, wout_h,
    n1_ref, qkv_ref, o_ref, lse_ref, orecv, wa, small, y1_ref, n2_ref, c_ref, dyx, win, wout,
    xall, wq, olow, tb_ref,
    xs, xr, ws, wr_, os_, or_, ds, dr, fs, fr, ls,
    *, ndp, nz, hg, hd, scale, experts,
):
    d = lax.axis_index("dp")
    z = lax.axis_index("z")
    c = lax.axis_index("core")
    span, model = xall.shape
    slots = x_ref.shape[1]
    block = 2 * slots
    width = hg * hd
    me = z * 2 + c
    part = wq_l.shape[0]
    hid = win.shape[2]
    own = d * 2 + c

    barrier = pltpu.get_barrier_semaphore()
    count = 0
    for k in range(ndp):
        for cc in range(2):
            if k or cc:
                pl.semaphore_signal(
                    barrier, inc=1, device_id_type=MESH,
                    device_id={"dp": xor(d, k), "z": z, "core": xor(c, cc)},
                )
                count += 1
    for k in range(1, 2 * nz):
        t = lax.rem(me + k, 2 * nz)
        tz = lax.div(t, 2)

        @pl.when(tz != z)
        def greet():
            pl.semaphore_signal(
                barrier, inc=1, device_id_type=MESH,
                device_id={"dp": d, "z": tz, "core": lax.rem(t, 2)},
            )
    pl.semaphore_wait(barrier, count + 2 * nz - 2)

    def x_copy(k):
        t = lax.rem(me + k, 2 * nz)
        tc = lax.rem(t, 2)
        rows = pl.ds(pl.multiple_of(me * slots, slots), slots)
        return remote(x_ref.at[tc], xall.at[rows, :], xs.at[k], xr.at[k], d, lax.div(t, 2), tc)

    for k in range(1, 2 * nz):
        x_copy(k).start()
    xall[pl.ds(pl.multiple_of(me * slots, slots), slots), :] = x_ref[c]

    def win_block(index):
        if len(win_h.shape) == 4:
            return win_h.at[index]
        return win_h.at[:, :, pl.ds(pl.multiple_of(index * hid, 128), hid)]

    def w_copy(k, which):
        peer = xor(d, k)
        rows = pl.ds(pl.multiple_of(d * part, part), part)
        if which == 0:
            pair = (wq_l, wq.at[rows, :])
        elif which == 1:
            pair = (wa_l, wa.at[rows, :])
        elif which == 2:
            pair = (small_l, small.at[d])
        else:
            pair = (win_block(peer * 2 + c), win.at[:, rows, :])
        return remote(*pair, ws.at[which, k], wr_.at[which, k], peer, z, c)

    for which in (2, 0, 1):
        for k in range(1, ndp):
            w_copy(k, which).start()
    rows_d = pl.ds(pl.multiple_of(d * part, part), part)
    wq[rows_d, :] = wq_l[...]
    wa[rows_d, :] = wa_l[...]
    small[pl.ds(d, 1)] = small_l[...][None]
    win_own = pltpu.make_async_copy(win_block(own), win.at[:, rows_d, :], ls.at[0])
    win_own.start()
    out_rows = pl.ds(pl.multiple_of(c * hid, 16), hid)
    wout_own = pltpu.make_async_copy(wout_h.at[:, out_rows, :], wout, ls.at[1])
    wout_own.start()
    for m in range(2):
        place = me * slots + lax.broadcasted_iota(jnp.int32, (slots, 1), 0)
        keep = place < len_ref[m]
        rows = pl.ds(m * slots, slots)
        dyx[own, rows, :model] = jnp.where(keep, cot_ref[m].astype(F32), 0.0).astype(BF16)
    dyx[own, :, model:] = route_ref[...]
    for head in range(hg):
        for delta in range(span // block):
            tb_ref[head, delta] = bias_tile(rd_ref, head, delta, span, block)

    for k in range(1, ndp):
        w_copy(k, 2).wait_recv()
        w_copy(k, 0).wait_recv()
    for k in range(1, ndp):
        w_copy(k, 3).start()

    def dy_copy(k):
        return remote(dyx.at[own], dyx.at[own], ds.at[k], dr.at[k], xor(d, k), z, c)

    def dy_pass(k):
        slot = dyx.at[xor(d, k) * 2 + c]
        return remote(slot, slot, fs.at[k], fr.at[k], d, z, 1 - c)

    dy_pass(0).start()
    for k in range(1, ndp):
        dy_copy(k).start()

    for k in range(1, 2 * nz):
        x_copy(k).wait_recv()
    gains = jnp.concatenate([small[i] for i in range(ndp)], axis=1)
    gain = gains[0:1, :]
    length = len_ref[c]
    for i in range(span // block):
        rows = slice(i * block, (i + 1) * block)
        x = xall[rows, :].astype(F32)
        n1 = (x * rms_scale(x) * gain).astype(BF16)
        n1_ref[rows, :] = n1
        qkv_ref[rows, :] = dot_nn(n1, wq[...]).astype(BF16)

    def o_copy(t):
        rows = pl.ds(t * slots, slots)
        return remote(
            olow.at[rows, :], orecv.at[z, c], os_.at[t], or_.at[me], d, t // 2, t % 2
        )

    def o_land(t):
        slot = orecv.at[t // 2, t % 2]
        return remote(slot, slot, os_.at[t], or_.at[t], d, t // 2, t % 2)

    lane = lax.broadcasted_iota(jnp.int32, (block, 128), 1)
    for i in range(span // block):
        rows = slice(i * block, (i + 1) * block)
        lse_all = jnp.zeros((block, 128), F32)
        outs = []
        for head in range(hg):
            cols = slice(head * hd, (head + 1) * hd)
            kcols = slice(width + head * hd, width + (head + 1) * hd)
            vcols = slice(2 * width + head * hd, 2 * width + (head + 1) * hd)
            q = qkv_ref[rows, cols]
            scores = []
            top = None
            for j in range(i + 1):
                keys = slice(j * block, (j + 1) * block)
                s = dot_nt(q, qkv_ref[keys, kcols]) * scale + tb_ref[head, i - j]
                s = jnp.where(allowed_tile(length, i * block, j * block, block), s, NEGATIVE)
                scores.append(s)
                peak = jnp.max(s, axis=-1, keepdims=True)
                top = peak if top is None else jnp.maximum(top, peak)
            total = jnp.zeros((block, 1), F32)
            accum = jnp.zeros((block, hd), F32)
            for j in range(i + 1):
                keys = slice(j * block, (j + 1) * block)
                weights = jnp.exp(scores[j] - top)
                total = total + jnp.sum(weights, axis=-1, keepdims=True)
                accum = accum + dot_nn(weights.astype(BF16), qkv_ref[keys, vcols])
            outs.append(accum / total)
            lse_all = jnp.where(lane == head, top + jnp.log(total), lse_all)
        out = jnp.concatenate(outs, axis=1)
        o_ref[rows, :] = out
        olow[rows, :] = out.astype(BF16)
        lse_ref[rows, :] = lse_all
        for t in (2 * i, 2 * i + 1):

            @pl.when(t != me)
            def away():
                o_copy(t).start()

            @pl.when(t == me)
            def stay():
                orecv[z, c] = olow[t * slots : (t + 1) * slots, :]

    for k in range(1, ndp):
        dy_copy(k).wait_recv()
        dy_pass(k).start()
        w_copy(k, 1).wait_recv()

    for t in range(2 * nz):

        @pl.when(t != me)
        def landed():
            o_land(t).wait_recv()

    gain_two = gains[1:2, :]
    for m in range(2):
        rows = slice(m * slots, (m + 1) * slots)
        y1 = x_ref[m].astype(F32)
        for g in range(nz):
            if g * width < model:
                y1 = y1 + dot_nn(orecv[g, m], wa[g * width : (g + 1) * width, :])
        n2 = (y1 * rms_scale(y1) * gain_two).astype(BF16)
        y1_ref[rows, :] = y1
        n2_ref[rows, :] = n2
        logits = dot_nt(n2, gains.astype(BF16))[:, 2 : 2 + experts]
        c_ref[rows, :] = gate_weights(logits, route_ref[rows, :].astype(F32), experts)

    for k in range(1, 2 * nz):
        x_copy(k).wait_send()
    for k in range(1, ndp):
        w_copy(k, 3).wait_recv()
        dy_pass(k).wait_recv()
        dy_pass(k).wait_send()
        dy_copy(k).wait_send()
        for which in range(4):
            w_copy(k, which).wait_send()
    dy_pass(0).wait()
    win_own.wait()
    wout_own.wait()
    for t in range(2 * nz):

        @pl.when(t != me)
        def sent():
            o_copy(t).wait_send()


def front(length, x, cot, route, rd, wq_l, wa_l, small_l, win_h, wout_h, ndp, nz, hg, hd, scale, experts, heads):
    slots, model = x.shape[1:]
    span = nz * 2 * slots
    width = hg * hd
    rows = 2 * slots
    hid = wout_h.shape[1] // 2
    any_spec = pl.BlockSpec(memory_space=pl.ANY)
    dma = pltpu.SemaphoreType.DMA
    shape = jax.ShapeDtypeStruct
    return pl.pallas_call(
        functools.partial(front_kernel, ndp=ndp, nz=nz, hg=hg, hd=hd, scale=scale, experts=experts),
        out_shape=(
            shape((span, model), BF16),
            shape((span, 3 * width), BF16),
            shape((span, width), F32),
            shape((span, 128), F32),
            shape((nz, 2, slots, width), BF16),
            shape((nz * width, model), BF16),
            shape((ndp,) + small_l.shape, F32),
            shape((rows, model), F32),
            shape((rows, model), BF16),
            shape((rows, experts), F32),
            shape((ndp * 2, rows, model + 128), BF16),
            shape((experts, model, hid), BF16),
            shape((experts, hid, model), BF16),
        ),
        in_specs=[pl.BlockSpec(memory_space=pltpu.SMEM)] + vmem_specs(7) + [any_spec] * 2,
        out_specs=tuple(vmem_specs(13)),
        scratch_shapes=[
            pltpu.VMEM((span, model), BF16),
            pltpu.VMEM((model, 3 * width), BF16),
            pltpu.VMEM((span, width), BF16),
            pltpu.VMEM((hg, span // rows, rows, rows), F32),
            dma((2 * nz,)), dma((2 * nz,)),
            dma((4, ndp)), dma((4, ndp)),
            dma((2 * nz,)), dma((2 * nz,)),
            dma((ndp,)), dma((ndp,)), dma((ndp,)), dma((ndp,)),
            dma((2,)),
        ],
        compiler_params=pltpu.CompilerParams(
            vmem_limit_bytes=VMEM_LIMIT, collective_id=0, has_side_effects=True
        ),
        name="front",
    )(length, x, cot, route, rd, wq_l, wa_l, small_l, win_h, wout_h)


def vmem_specs(count):
    return [pl.BlockSpec(memory_space=pltpu.VMEM)] * count


def skew_sum(tile):
    rows, wide = tile.shape
    while rows > 1:
        half = rows // 2
        tile = tile[:half] + pltpu.roll(tile[half:], wide - half, 1)
        rows = half
    return tile


def attend_back_kernel(
    len_ref, n1_ref, qkv_ref, o_ref, lse_ref, do_ref, w_ref, rd_ref,
    dn1_ref, dw_ref, dd_ref, tb_ref, dt_ref, dacc_ref, dlow_ref,
    *, hg, hd, block, scale,
):
    span = n1_ref.shape[0]
    count = span // block
    width = hg * hd
    length = len_ref[0]
    for head in range(hg):
        for delta in range(count):
            tb_ref[head, delta] = bias_tile(rd_ref, head, delta, span, block)
    dt_ref[...] = jnp.zeros_like(dt_ref)
    dacc_ref[...] = jnp.zeros_like(dacc_ref)
    for i in range(count):
        rows = slice(i * block, (i + 1) * block)
        for head in range(hg):
            cols = slice(head * hd, (head + 1) * hd)
            kcols = slice(width + head * hd, width + (head + 1) * hd)
            vcols = slice(2 * width + head * hd, 2 * width + (head + 1) * hd)
            q = qkv_ref[rows, cols]
            do = do_ref[rows, cols]
            delta_sum = jnp.sum(do.astype(F32) * o_ref[rows, cols], axis=-1, keepdims=True)
            lse = lse_ref[rows, head : head + 1]
            dq = jnp.zeros((block, hd), F32)
            for j in range(i + 1):
                keys = slice(j * block, (j + 1) * block)
                k = qkv_ref[keys, kcols]
                s = dot_nt(q, k) * scale + tb_ref[head, i - j]
                p = jnp.exp(s - lse)
                p = jnp.where(allowed_tile(length, i * block, j * block, block), p, 0.0)
                dp = dot_nt(do, qkv_ref[keys, vcols])
                ds = (p * (dp - delta_sum)).astype(BF16)
                dt_ref[head, i - j] += ds.astype(F32)
                dq = dq + dot_nn(ds, k)
                dacc_ref[keys, kcols] += dot_tn(ds, q)
                dacc_ref[keys, vcols] += dot_tn(p.astype(BF16), do)
            dacc_ref[rows, cols] = dq
    for i in range(count):
        rows = slice(i * block, (i + 1) * block)
        dlow_ref[rows, : 2 * width] = (dacc_ref[rows, : 2 * width] * scale).astype(BF16)
        dlow_ref[rows, 2 * width :] = dacc_ref[rows, 2 * width :].astype(BF16)
        dn1_ref[rows, :] = dot_nt(dlow_ref[rows, :], w_ref[...]).astype(BF16)
    dw_ref[...] = dot_tn(n1_ref[...], dlow_ref[...]).astype(dw_ref.dtype)
    dd_ref[...] = jnp.zeros_like(dd_ref)
    for head in range(hg):
        for delta in range(count):
            low = span - (delta + 1) * block
            tile = jnp.concatenate(
                [dt_ref[head, delta], jnp.zeros((block, block), F32)], axis=1
            )
            row = pltpu.roll(skew_sum(tile), block - 1, 1)
            dd_ref[head : head + 1, low : low + 2 * block] += row


def attend_back(length, n1, qkv, o, lse, do, w, rd, hg, hd, scale):
    span, model = n1.shape
    block = 256
    width = hg * hd
    return pl.pallas_call(
        functools.partial(attend_back_kernel, hg=hg, hd=hd, block=block, scale=scale),
        out_shape=(
            jax.ShapeDtypeStruct((span, model), BF16),
            jax.ShapeDtypeStruct((model, 3 * width), BF16),
            jax.ShapeDtypeStruct((hg, span + block), F32),
        ),
        in_specs=[pl.BlockSpec(memory_space=pltpu.SMEM)] + vmem_specs(7),
        out_specs=tuple(vmem_specs(3)),
        scratch_shapes=[
            pltpu.VMEM((hg, span // block, block, block), F32),
            pltpu.VMEM((hg, span // block, block, block), F32),
            pltpu.VMEM((span, 3 * width), F32),
            pltpu.VMEM((span, 3 * width), BF16),
        ],
        compiler_params=pltpu.CompilerParams(vmem_limit_bytes=VMEM_LIMIT),
        name="attend_back",
    )(length, n1, qkv, o, lse, do, w, rd)


def gelu_parts(hidden):
    density = jnp.exp(-0.5 * hidden * hidden)
    t = 1.0 / (1.0 + (0.3275911 * 0.7071067811865476) * jnp.abs(hidden))
    poly = 1.061405429 * t - 1.453152027
    poly = poly * t + 1.421413741
    poly = poly * t - 0.284496736
    poly = poly * t + 0.254829592
    tail = 0.5 * poly * t * density
    phi = jnp.where(hidden >= 0.0, 1.0 - tail, tail)
    return hidden * phi, phi + hidden * density * 0.3989422804014327


def expert_kernel(
    n2_ref, dy_ref, c_ref, win_ref, wout_ref, y_ref, dn2_ref, dg_ref, dwin_ref, dwout_ref,
    awin_ref, awout_ref, *, experts, hidden_count,
):
    step = pl.program_id(0)
    last = pl.num_programs(0) - 1

    @pl.when(step == 0)
    def start():
        awin_ref[...] = jnp.zeros_like(awin_ref)
        awout_ref[...] = jnp.zeros_like(awout_ref)

    n2 = n2_ref[...]
    dy = dy_ref[...]
    c = c_ref[...]
    dgs = []
    y = None
    dn2 = None
    for e in range(experts):
        part = slice(e * hidden_count, (e + 1) * hidden_count)
        weight = c[:, e : e + 1]
        hidden = dot_nn(n2, win_ref[:, part])
        active, slope = gelu_parts(hidden)
        back = dot_nt(dy, wout_ref[part, :])
        dgs.append(jnp.sum(active * back, axis=-1, keepdims=True))
        mixed = (active * weight).astype(BF16)
        d_hidden = (back * weight * slope).astype(BF16)
        term = dot_nn(mixed, wout_ref[part, :])
        y = term if y is None else y + term
        term = dot_nt(d_hidden, win_ref[:, part])
        dn2 = term if dn2 is None else dn2 + term
        awout_ref[part, :] += dot_tn(mixed, dy)
        awin_ref[:, part] += dot_tn(n2, d_hidden)
    y_ref[...] = y.astype(BF16)
    dn2_ref[...] = dn2.astype(BF16)
    dg_ref[...] = jnp.concatenate(dgs, axis=1)

    @pl.when(step == last)
    def finish():
        dwin_ref[...] = awin_ref[...].astype(BF16)
        dwout_ref[...] = awout_ref[...].astype(BF16)


def expert_layer(n2, dy, c, win, wout, experts):
    count, model = n2.shape
    block = 256
    hidden_count = win.shape[1] // experts
    rows = pl.BlockSpec((block, model), lambda i: (i, 0))
    few = pl.BlockSpec((block, experts), lambda i: (i, 0))
    whole = pl.BlockSpec(memory_space=pltpu.VMEM)
    return pl.pallas_call(
        functools.partial(expert_kernel, experts=experts, hidden_count=hidden_count),
        out_shape=(
            jax.ShapeDtypeStruct((count, model), BF16),
            jax.ShapeDtypeStruct((count, model), BF16),
            jax.ShapeDtypeStruct((count, experts), F32),
            jax.ShapeDtypeStruct(win.shape, BF16),
            jax.ShapeDtypeStruct(wout.shape, BF16),
        ),
        grid=(count // block,),
        in_specs=[rows, rows, few, whole, whole],
        out_specs=(rows, rows, few, whole, whole),
        scratch_shapes=[pltpu.VMEM(win.shape, F32), pltpu.VMEM(wout.shape, F32)],
        compiler_params=pltpu.CompilerParams(vmem_limit_bytes=VMEM_LIMIT),
        name="experts",
    )(n2, dy, c, win, wout)


def local(
    tokens, lengths, routes, rel_table, rel_bias, cotangent, w_qkv, w_attn, w_router,
    gain_attn, gain_moe, w_expert_in, w_expert_out, *, ndp, nz,
):
    micro, _, slots, model = tokens.shape
    span = rel_table.shape[0]
    buckets_count, heads = rel_bias.shape
    hd = model // heads
    scale = hd ** (-0.5)
    experts = w_expert_in.shape[0]
    ff = w_expert_in.shape[2]
    hg = -(-heads // nz)
    pad_heads = hg * nz - heads
    width = hg * hd
    z = lax.axis_index("z")
    core = lax.axis_index("core")
    x_loc = tokens[:, 0]
    wq = w_qkv.reshape(-1, 3, heads, hd)
    wq = jnp.pad(wq, ((0, 0), (0, 0), (0, pad_heads), (0, 0)))
    wq = lax.dynamic_slice_in_dim(wq, z * hg, hg, 2).reshape(-1, 3 * width)
    share = ff // (ndp * nz * 2)
    hidden_count = nz * share
    small = jnp.concatenate([gain_attn[None], gain_moe[None], w_router.T], axis=0).astype(F32)
    small = jnp.pad(small, ((0, 8 - small.shape[0]), (0, 0)))
    route = jnp.pad(routes.reshape(micro * slots, 2).astype(BF16), ((0, 0), (0, 126)))

    turned = rel_table[::-1]
    onehot = (turned[:, None] == jnp.arange(buckets_count, dtype=jnp.int32)[None, :]).astype(F32)
    bias_rows = jnp.pad(rel_bias.T, ((0, pad_heads), (0, 0)))
    bias_rows = lax.dynamic_slice_in_dim(bias_rows, z * hg, hg, 0)
    rd = lax.dot_general(bias_rows, onehot, (((1,), (1,)), ((), ())), precision=HIGH)
    rd = jnp.pad(rd, ((0, 0), (0, 2 * slots)))
    length = lax.dynamic_index_in_dim(lengths[:, 0], core, 0, keepdims=True)

    w_in = w_expert_in
    if hidden_count % 128:
        w_in = w_in.reshape(experts, -1, ndp * 2, hidden_count).transpose(2, 0, 1, 3)
    n1, qkv, o, lse, orecv, wa, small, y1, n2, c, dyx, win, wout = front(
        lengths[:, 0], x_loc, cotangent[:, 0], route, rd, wq, w_attn, small,
        w_in, w_expert_out, ndp, nz, hg, hd, scale, experts, heads,
    )
    olow = orecv.transpose(1, 2, 0, 3).reshape(micro * slots, nz * width)[:, :model]
    gains = small.transpose(1, 0, 2).reshape(8, model)
    ga = gains[0]
    gm = gains[1]
    wr = gains[2 : 2 + experts].astype(BF16).T
    wa = wa[:model]
    x = x_loc.reshape(micro * slots, model).astype(F32)
    own = lax.axis_index("dp") * 2 + core
    dy = dyx[:, :, :model].reshape(-1, model)
    dy_loc = lax.dynamic_index_in_dim(dyx, own, 0, keepdims=False)[:, :model]
    wq = lax.all_gather(wq, "dp", axis=0, tiled=True)
    win = win.transpose(1, 0, 2).reshape(model, experts * hidden_count)
    wout = wout.reshape(experts * hidden_count, model)
    r2 = rms_scale(y1)
    z2 = y1 * r2
    gain_two = gm
    logits = dot_nn(n2, wr)
    chosen = (
        routes.reshape(micro * slots, 2)[:, :, None] == jnp.arange(experts)[None, None, :]
    ).astype(F32)
    routed = jnp.sum(chosen * logits[:, None, :], axis=-1)
    gates = jax.nn.softmax(routed, axis=-1)

    n2_all = lax.all_gather(n2, PLANE, axis=0, tiled=True)
    c_all = lax.all_gather(c, PLANE, axis=0, tiled=True)
    y_part, dn2_part, dg_part, dwin, dwout = expert_layer(n2_all, dy, c_all, win, wout, experts)
    y = lax.psum_scatter(y_part, PLANE, scatter_dimension=0, tiled=True)
    dn2 = lax.psum_scatter(dn2_part, PLANE, scatter_dimension=0, tiled=True).astype(F32)
    dg = lax.psum_scatter(dg_part, PLANE, scatter_dimension=0, tiled=True)
    output = (y1 + y.astype(F32)).astype(BF16)

    d_routed_gate = jnp.sum(chosen * dg[:, None, :], axis=-1)
    d_routed = gates * (d_routed_gate - jnp.sum(gates * d_routed_gate, axis=-1, keepdims=True))
    d_logits = jnp.sum(chosen * d_routed[:, :, None], axis=1).astype(BF16)
    g_router = dot_tn(n2, d_logits)
    dn2 = dn2 + dot_nt(d_logits, wr)
    d_norm, g_gain_moe = norm_back(dn2, z2, gain_two, r2)
    dy1 = dy_loc.astype(F32) + d_norm
    dbr = dy1.astype(BF16)
    g_attn = dot_tn(olow, dbr).astype(BF16)
    do = dot_nt(dbr, wa).astype(BF16)
    do = jnp.pad(do, ((0, 0), (0, nz * width - model)))
    do = do.reshape(2, slots, nz, width).transpose(2, 0, 1, 3).reshape(nz * 2, slots, width)
    do = lax.all_to_all(do, COLUMN, 0, 0, tiled=True).reshape(span, width)

    dn1_part, g_qkv, dd = attend_back(length, n1, qkv, o, lse, do, wq, rd, hg, hd, scale)
    dn1 = dn1_part.reshape(nz, 1, 2 * slots, model)
    dn1 = lax.psum_scatter(dn1, "z", scatter_dimension=0, tiled=True)[0]
    dn1 = lax.all_to_all(dn1, "core", 1, 0, tiled=True).reshape(micro * slots, model).astype(F32)
    r1 = rms_scale(x)
    z1 = x * r1
    d_norm, g_gain_attn = norm_back(dn1, z1, ga, r1)
    d_tokens = (dy1 + d_norm).astype(BF16)

    piece = model // (ndp * nz * 2)
    g_out = dwout.reshape(experts, 1, nz // 2, 2, share, model)
    spread = jnp.zeros((experts, 2, nz // 2, 2, share, model), BF16)
    g_out = lax.dynamic_update_slice_in_dim(spread, g_out, core, 1)
    g_out = g_out.reshape(experts, nz * 2, share, model)
    g_out = lax.psum_scatter(g_out, COLUMN, scatter_dimension=1, tiled=True)
    g_out = g_out.reshape(experts, share, model).astype(F32)
    g_in = dwin.reshape(ndp, nz, 2, piece, experts * hidden_count)
    g_in = lax.psum_scatter(g_in, "z", scatter_dimension=1, tiled=True)
    g_in = g_in.reshape(ndp * 2, piece, experts * hidden_count)
    g_in = lax.all_to_all(g_in, PLANE, 0, 0, tiled=True)
    g_in = g_in.reshape(ndp, 2, piece, experts, hidden_count).transpose(3, 2, 0, 1, 4)
    g_in = g_in.reshape(experts, piece, ff).astype(F32)
    g_qkv = g_qkv.reshape(ndp, nz, 2, piece, 3 * width).transpose(0, 2, 1, 3, 4)
    g_qkv = g_qkv.reshape(ndp * 2, nz, piece, 3 * width)
    g_qkv = lax.psum_scatter(g_qkv, PLANE, scatter_dimension=0, tiled=True)[0]
    g_qkv = lax.all_to_all(g_qkv, "z", 0, 0, tiled=True)
    g_qkv = g_qkv.reshape(nz, piece, 3, width).transpose(1, 2, 0, 3).reshape(piece, 3, nz * width)
    g_qkv = g_qkv[:, :, :model].reshape(piece, 3 * model).astype(F32)
    g_attn = lax.psum_scatter(g_attn, EVERY, scatter_dimension=0, tiled=True).astype(F32)

    d_dist = dd[:, :span]
    g_bias = lax.dot_general(onehot, d_dist, (((0,), (1,)), ((), ())), precision=HIGH)
    spread = jnp.zeros((buckets_count, nz * hg), F32)
    g_bias = lax.dynamic_update_slice_in_dim(spread, g_bias, z * hg, 1)[:, :heads].reshape(-1)
    small = jnp.concatenate([g_router.reshape(-1), g_gain_attn, g_gain_moe, g_bias])
    small = lax.psum(small, EVERY)
    place = (lax.axis_index("dp") * nz + z) * 2 + core

    def own(first, count, rows):
        return lax.dynamic_slice_in_dim(small, first + place * rows, rows, 0)

    g_router = own(0, 0, piece * experts).reshape(piece, experts)
    g_gain_attn = own(model * experts, 0, piece)
    g_gain_moe = own(model * (experts + 1), 0, piece)
    each = buckets_count * heads // (ndp * nz * 2)
    g_bias = own(model * (experts + 2), 0, each)
    return (
        output.reshape(micro, 1, slots, model),
        d_tokens.reshape(micro, 1, slots, model),
        g_qkv, g_attn, g_router, g_gain_attn, g_gain_moe, g_in, g_out, g_bias,
    )


def solution(mesh):
    devices = mesh.devices
    ndp, nctx = devices.shape
    nz = nctx // 2
    sub = jax.sharding.Mesh(devices.reshape(ndp, nz, 2), EVERY)
    in_specs = (
        P(None, "dp", COLUMN, None),
        P(None, "dp"),
        P(None, "dp", COLUMN, None),
        P(),
        P(),
        P(None, "dp", COLUMN, None),
        P("dp", None),
        P("dp", None),
        P("dp", None),
        P("dp"),
        P("dp"),
        P(None, "dp", None),
        P(None, "dp", None),
    )
    out_specs = (
        P(None, "dp", COLUMN, None),
        P(None, "dp", COLUMN, None),
        P(EVERY, None),
        P(EVERY, None),
        P(EVERY, None),
        P(EVERY),
        P(EVERY),
        P(None, EVERY, None),
        P(None, EVERY, None),
        P(EVERY),
    )
    return jax.shard_map(
        functools.partial(local, ndp=ndp, nz=nz), mesh=sub,
        in_specs=in_specs, out_specs=out_specs, check_vma=False,
    )
```
